256 devices in a mesh: blk: 32 (over y_hi, z, core), lag: 8 (over y_lo, x).
Axes of the slice: x: 4, y: 4 (y_hi: 2, y_lo: 2; y = y_hi * 2 + y_lo), z: 8, core: 2. Of those that a mesh axis runs over, the one named last changes fastest.
Arguments:
- waves: bfloat16 [1024, 4096], P('blk', 'lag'), may hold values from -6 to 6
- dest_of: int32 [1024], P('blk'), may hold values from 0 to 1023, as said below
- pair_mask: int32 [1024, 1024], P('blk'), may hold values from 0 to 1, as said below
Outputs:
- xcorr: float32 [1024, 512, 1024], P('blk', 'lag')
The draws below stay inside these ranges and needn't reach their ends.
Inputs may be any that keep to these rules, and one draw needn't show every extreme that they name: dest_of is a permutation; position p belongs to owner p // 32; each owner receives exactly 1 stations from each source block of 32 stations, and those from source block s take positions s * 1 to s + 1 - 1 of the owner's tile. `pair_mask`: whole blocks of 32 x 32 aligned positions may be zero.
All inputs are finite; a program needn't handle non-finite values.
Results may differ from the reference program's by a relative error of at most 0.0041.
Values may be sent and summed in bfloat16 or wider, within the bound.
A program may use at most 192 MiB of HBM per device.

```python
import math
import jax
import jax.numpy as jnp
from jax import lax

TILE = 32
LAGS = 512
STATIONS = 1024
NT = 4096
PER_SRC = 1


def draw_dest_of(key, part):
    blocks = STATIONS // TILE
    keys = jax.random.split(jax.random.fold_in(key, 7), blocks)
    orders = jax.vmap(lambda single: jax.random.permutation(single, TILE))(keys).astype(jnp.int32)
    source = jnp.arange(blocks, dtype=jnp.int32)[:, None]
    placed = orders // PER_SRC * TILE + source * PER_SRC + orders % PER_SRC
    return placed.reshape(STATIONS).astype(jnp.int32)


def draw_pair_mask(key, part):
    blocks = STATIONS // TILE
    first, second, third = jax.random.split(jax.random.fold_in(key, 11), 3)
    level = jax.random.randint(first, (blocks, 1), 1, 5)
    active = (jax.random.randint(second, (blocks, blocks), 0, 4) < level).astype(jnp.int32)
    tiles = jnp.repeat(jnp.repeat(active, TILE, axis=0), TILE, axis=1)
    entries = jax.random.randint(third, (STATIONS, STATIONS), 0, 2)
    return (tiles * entries).astype(jnp.int32)


def shard_levels(stream_key, extent, cuts, smallest, high):
    gain, own = 1.0, jax.random.fold_in(stream_key, 6)
    for position, parts in cuts:
        draws = jnp.exp(jax.random.uniform(jax.random.fold_in(own, position), (parts,), jnp.float32, smallest / len(cuts), high / len(cuts)))
        gain = gain * jnp.repeat(draws, extent[position] // parts).reshape([-1 if axis == position else 1 for axis in range(len(extent))])
    return gain


def noise(stream_key, dims, scale, bound, cuts=(), kind=jnp.bfloat16):
    loudness = shard_levels(stream_key, dims, cuts, -0.22, 0.18) if cuts else 1.0
    result = jax.random.normal(stream_key, dims, jnp.float32) * scale * loudness
    return jnp.minimum(jnp.maximum(result, -bound), bound).astype(kind)


def setup_inputs(seed: int = 0) -> dict:
    splits = jax.random.split(jax.random.key(seed), 4)
    return {
        "waves": noise(splits[0], (STATIONS, NT), 1.0, 6.0, ((0, 32), (1, 8))),
        "dest_of": draw_dest_of(jax.random.fold_in(splits[3], 71), 0),
        "pair_mask": draw_pair_mask(jax.random.fold_in(splits[3], 71), 0),
    }


EPS = 1e-06

def reference(waves, dest_of, pair_mask):
    clustered = jnp.zeros_like(waves).at[dest_of].set(waves)
    floats = clustered.astype(jnp.float32)
    mean_square = lax.optimization_barrier(jnp.mean(floats * floats, axis=1, keepdims=True))
    normed = (floats * lax.rsqrt(mean_square + EPS)).astype(jnp.bfloat16)
    normed_wide = normed.astype(jnp.float32)
    padded = jnp.pad(normed_wide, ((0, 0), (LAGS, LAGS)))
    lag_block = math.gcd(LAGS, 64)
    row_block = math.gcd(STATIONS, 32)
    lag_count = LAGS // lag_block
    row_count = STATIONS // row_block
    scaling = 1.0 / math.sqrt(NT)

    def one_block(index):
        lag_index = index // row_count
        row_index = index % row_count
        lag_start = (lag_index * lag_block - LAGS // 2).astype(jnp.int32)
        rows_here = lax.dynamic_slice_in_dim(padded, (row_index * row_block).astype(jnp.int32), row_block, 0)

        def shifted(shift_count):
            return lax.dynamic_slice_in_dim(rows_here, (LAGS - lag_start - shift_count).astype(jnp.int32), NT, 1)
        stacked = jax.vmap(shifted)(jnp.arange(lag_block, dtype=jnp.int32))
        hankel = jnp.transpose(stacked, (2, 1, 0)).reshape(NT, row_block * lag_block)
        product = jnp.dot(normed_wide, hankel, preferred_element_type=jnp.float32)
        product = product.reshape(STATIONS, row_block, lag_block)
        return jnp.transpose(product, (1, 2, 0)) * scaling
    blocks = lax.map(one_block, jnp.arange(lag_count * row_count, dtype=jnp.int32))
    blocks = blocks.reshape(lag_count, row_count, row_block, lag_block, STATIONS)
    blocks = jnp.transpose(blocks, (1, 2, 0, 3, 4)).reshape(STATIONS, LAGS, STATIONS)
    return blocks * pair_mask[:, None, :].astype(jnp.float32)
```

```python
import functools

import jax
import jax.numpy as jnp
from jax import lax
from jax.sharding import PartitionSpec as P
import jax.experimental.pallas as pl
import jax.experimental.pallas.tpu as pltpu

EPS = 1e-06
LAGS = 512
MESH = pl.DeviceIdType.MESH
SIZES = {"x": 4, "y": 4, "z": 8}
PARTS = ((0, 1, "xyz"), (1, 1, "yzx"), (2, 2, "zxy"))


def gather_kernel(w_ref, d_ref, o_ref, send, land, held, a_send, a_recv, r_send, r_recv, s_send, s_recv, out_sem):
    b, g = lax.axis_index("blk"), lax.axis_index("lag")
    core, cz, yh = b % 2, (b // 2) % 8, b // 16
    yl, cx = g // 4, g % 4
    here = {"x": cx, "y": yh * 2 + yl, "z": cz}

    def device(pos, c):
        return ((pos["y"] // 2 * 8 + pos["z"]) * 2 + c, pos["y"] % 2 * 4 + pos["x"])

    def shifted(axis, by):
        n = SIZES[axis]
        return lax.rem(here[axis] + (by + n), n)

    def neighbour(axis, by):
        return device({**here, axis: shifted(axis, by)}, core)

    sibling = device(here, 1 - core)

    def slot(c, where, part, rows=slice(0, 32)):
        first, count, _ = PARTS[part]
        y = where["y"]
        return held.at[
            slice(None) if y is None else y % 2,
            slice(None) if where["x"] is None else where["x"],
            pl.ds(first, count),
            slice(None) if y is None else y // 2,
            slice(None) if where["z"] is None else where["z"],
            c,
            pl.ds(rows.start, rows.stop - rows.start),
        ]

    barrier = pltpu.get_barrier_semaphore()

    def greet_blk(i, _):
        pl.semaphore_signal(barrier, inc=1, device_id=(lax.rem(b + i, 32), g), device_id_type=MESH)
        return 0

    lax.fori_loop(1, 32, greet_blk, 0)
    for axis in "xy":
        for by in (1, -1):
            pl.semaphore_signal(barrier, inc=1, device_id=neighbour(axis, by), device_id_type=MESH)

    owner = d_ref[...] // 32
    pick = (lax.broadcasted_iota(jnp.int32, (32, 32), 0) == owner).astype(jnp.bfloat16)
    ordered = jnp.dot(pick, w_ref[...], preferred_element_type=jnp.float32)
    for k in range(4):
        send[:, k, :] = ordered[:, 128 * k : 128 * k + 128]
    pl.semaphore_wait(barrier, 35)

    def put(i, _):
        to = lax.rem(b + i, 32)
        pltpu.make_async_remote_copy(
            src_ref=send.at[to], dst_ref=land.at[b], send_sem=a_send, recv_sem=a_recv,
            device_id=(to, g), device_id_type=MESH,
        ).start()
        return 0

    lax.fori_loop(1, 32, put, 0)
    land[b] = send[b]
    every = pltpu.make_async_remote_copy(
        src_ref=send.at[pl.ds(0, 31)], dst_ref=land.at[pl.ds(0, 31)], send_sem=a_send, recv_sem=a_recv,
        device_id=sibling, device_id_type=MESH,
    )
    every.wait_recv()
    for k in range(4):
        held[yl, cx, k, yh, cz, core] = land[:, k, :].astype(jnp.bfloat16)

    pending, sibling_pending = [], []

    def across(part, where, rows, index):
        mine = slot(core, where, part, rows)
        copy = pltpu.make_async_remote_copy(
            src_ref=mine, dst_ref=mine, send_sem=s_send.at[index], recv_sem=s_recv.at[index],
            device_id=sibling, device_id_type=MESH,
        )
        copy.start()
        pending.append(copy)
        theirs = slot(1 - core, where, part, rows)
        sibling_pending.append(
            pltpu.make_async_remote_copy(
                src_ref=theirs, dst_ref=theirs, send_sem=s_send.at[index], recv_sem=s_recv.at[index],
                device_id=sibling, device_id_type=MESH,
            )
        )

    steps = []
    for part, (_, _, order) in enumerate(PARTS):
        mine = []
        for phase, axis in enumerate(order):
            for step in range(1, SIZES[axis] // 2 + 1):
                mine.append((phase, axis, step))
        steps.append(mine)

    def where_of(part, phase, at):
        order = PARTS[part][2]
        where = {}
        for position, axis in enumerate(order):
            where[axis] = None if position < phase else (at if position == phase else here[axis])
        return where

    def rows_of(axis, step, way):
        if step < SIZES[axis] // 2:
            return slice(0, 32)
        return slice(0, 16) if way > 0 else slice(16, 32)

    for part in range(len(PARTS)):
        across(part, here, slice(0, 32), part * 17)
    for t in range(9):
        for part in range(len(PARTS)):
            if t > 0:
                phase, axis, step = steps[part][t - 1]
                for side, way in enumerate((1, -1)):
                    index = part * 17 + 1 + 2 * (t - 1) + side
                    rows = rows_of(axis, step, way)
                    where = where_of(part, phase, shifted(axis, -way * step))
                    mine = slot(core, where, part, rows)
                    pltpu.make_async_remote_copy(
                        src_ref=mine, dst_ref=mine, send_sem=r_send.at[index], recv_sem=r_recv.at[index],
                        device_id=sibling, device_id_type=MESH,
                    ).wait_recv()
            if t < 8:
                phase, axis, step = steps[part][t]
                for side, way in enumerate((1, -1)):
                    index = part * 17 + 1 + 2 * t + side
                    mine = slot(core, where_of(part, phase, shifted(axis, -way * (step - 1))), part, rows_of(axis, step, way))
                    copy = pltpu.make_async_remote_copy(
                        src_ref=mine, dst_ref=mine, send_sem=r_send.at[index], recv_sem=r_recv.at[index],
                        device_id=neighbour(axis, way), device_id_type=MESH,
                    )
                    copy.start()
                    pending.append(copy)
            if t > 0:
                phase, axis, step = steps[part][t - 1]
                for side, way in enumerate((1, -1)):
                    index = part * 17 + 1 + 2 * (t - 1) + side
                    across(part, where_of(part, phase, shifted(axis, -way * step)), rows_of(axis, step, way), index)
    for copy in sibling_pending:
        copy.wait_recv()
    out = pltpu.make_async_copy(held, o_ref, out_sem)
    out.start()
    every.wait_send()
    for copy in pending:
        copy.wait_send()
    out.wait()


def gather(waves, dest_of):
    count = 17 * len(PARTS)
    return pl.pallas_call(
        gather_kernel,
        out_shape=jax.ShapeDtypeStruct((2, 4, 4, 2, 8, 2, 32, 128), jnp.bfloat16),
        in_specs=[pl.BlockSpec(memory_space=pltpu.VMEM)] * 2,
        out_specs=pl.BlockSpec(memory_space=pl.ANY),
        scratch_shapes=[
            pltpu.VMEM((32, 4, 128), jnp.float32),
            pltpu.VMEM((32, 4, 128), jnp.float32),
            pltpu.VMEM((2, 4, 4, 2, 8, 2, 32, 128), jnp.bfloat16),
            pltpu.SemaphoreType.DMA,
            pltpu.SemaphoreType.DMA,
            pltpu.SemaphoreType.DMA((count,)),
            pltpu.SemaphoreType.DMA((count,)),
            pltpu.SemaphoreType.DMA((count,)),
            pltpu.SemaphoreType.DMA((count,)),
            pltpu.SemaphoreType.DMA,
        ],
        compiler_params=pltpu.CompilerParams(
            collective_id=0, has_side_effects=True, vmem_limit_bytes=32 * 2**20
        ),
    )(waves, dest_of)


def correlate_kernel(e_ref, g_ref, m_ref, o_ref, h_ref):
    @pl.when(pl.program_id(0) == 0)
    def _():
        def build(a, _):
            x = jnp.broadcast_to(e_ref[pl.ds(a, 1), :], (8, e_ref.shape[1]))
            for q in range(4):
                y0 = pltpu.roll(x, 16 * q, 1, stride=1, stride_axis=0)
                y1 = pltpu.roll(x, 16 * q + 8, 1, stride=1, stride_axis=0)
                y = jnp.concatenate([y0[:, 128:], y1[:, 128:]], 0).astype(h_ref.dtype)
                h_ref[pl.ds(pl.multiple_of(a * 64 + 16 * q, 16), 16), :] = y
            return 0

        lax.fori_loop(0, 32, build, 0)

    total = jnp.zeros((256, 128), jnp.float32)
    for k in range(32):
        wide = g_ref[k].astype(jnp.float32)
        total += wide * wide
    dims = (((1,), (1,)), ((), ()))
    square = lax.dot_general(
        jnp.ones((8, 128), jnp.float32), total, dims,
        precision=lax.Precision.HIGHEST, preferred_element_type=jnp.float32,
    )[:1]
    scale = lax.rsqrt(square * (1.0 / 4096) + EPS) * (1.0 / 64)

    def rows(m, _):
        r = pl.multiple_of(m * 1024, 1024)
        right = jnp.concatenate([g_ref[k] for k in range(32)], axis=1)
        acc = lax.dot_general(h_ref[pl.ds(r, 1024), :], right, dims, preferred_element_type=jnp.float32)
        for q in range(16):
            a = m * 16 + q
            o_ref[a] = acc[64 * q : 64 * q + 64] * (m_ref[pl.ds(a, 1), :].astype(jnp.float32) * scale)
        return 0

    lax.fori_loop(0, 2, rows, 0)


def correlate(shift, everyone, pair_mask):
    return pl.pallas_call(
        correlate_kernel,
        grid=(4,),
        out_shape=jax.ShapeDtypeStruct((32, 64, 1024), jnp.float32),
        in_specs=[
            pl.BlockSpec((32, 4224), lambda n: (0, 0)),
            pl.BlockSpec((32, 256, 128), lambda n: (0, n, 0)),
            pl.BlockSpec((32, 256), lambda n: (0, n)),
        ],
        out_specs=pl.BlockSpec((32, 64, 256), lambda n: (0, 0, n)),
        scratch_shapes=[pltpu.VMEM((2048, 4096), jnp.bfloat16)],
        compiler_params=pltpu.CompilerParams(vmem_limit_bytes=48 * 2**20),
    )(shift, everyone, pair_mask)


def body(waves, dest_of, pair_mask):
    everyone = gather(waves, dest_of[None, :]).reshape(32, 1024, 128)
    own = lax.dynamic_slice_in_dim(everyone, lax.axis_index("blk") * 32, 32, 1)
    own = own.transpose(1, 0, 2).reshape(32, 4096).astype(jnp.float32)
    mean_square = jnp.mean(own * own, axis=1, keepdims=True)
    normed = (own * lax.rsqrt(mean_square + EPS)).astype(jnp.bfloat16).astype(jnp.float32)
    padded = jnp.pad(normed, ((0, 0), (512, 512)))
    shift = lax.dynamic_slice_in_dim(padded, 640 - 64 * lax.axis_index("lag"), 4224, 1)
    return correlate(shift, everyone, pair_mask)


def solution(mesh):
    in_specs = (P("blk", "lag"), P("blk"), P("blk", None))
    out_specs = P("blk", "lag", None)
    return jax.shard_map(body, mesh=mesh, in_specs=in_specs, out_specs=out_specs, check_vma=False)
```

```python
import functools

import jax
import jax.numpy as jnp
from jax import lax
from jax.sharding import PartitionSpec as P
import jax.experimental.pallas as pl
import jax.experimental.pallas.tpu as pltpu

EPS = 1e-06
LAGS = 512
MESH = pl.DeviceIdType.MESH
SIZES = {"x": 4, "y": 4, "z": 8}


def gather_kernel(w_ref, d_ref, held, send, land, a_send, a_recv, s_sem, r_sem):
    b, g = lax.axis_index("blk"), lax.axis_index("lag")
    core, cz, yh = b % 2, (b // 2) % 8, b // 16
    yl, cx = g // 4, g % 4
    here = {"x": cx, "y": yh * 2 + yl, "z": cz}
    everywhere, upper, lower = pl.ds(0, 32), pl.ds(0, 16), pl.ds(16, 16)

    def device(pos, c):
        return ((pos["y"] // 2 * 8 + pos["z"]) * 2 + c, pos["y"] % 2 * 4 + pos["x"])

    def shifted(axis, by):
        n = SIZES[axis]
        return lax.rem(here[axis] + (by + n), n)

    def neighbour(axis, by):
        return device({**here, axis: shifted(axis, by)}, core)

    sibling = device(here, 1 - core)

    def slot(c, tiles, rows, x=None, y=None, z=None, y_low=None):
        low = slice(None) if y is None else y % 2
        return held.at[
            low if y_low is None else y_low,
            slice(None) if x is None else x,
            tiles,
            slice(None) if y is None else y // 2,
            slice(None) if z is None else z,
            c,
            rows,
        ]

    barrier = pltpu.get_barrier_semaphore()

    def greet_blk(i, _):
        pl.semaphore_signal(barrier, inc=1, device_id=(lax.rem(b + i, 32), g), device_id_type=MESH)
        return 0

    lax.fori_loop(1, 32, greet_blk, 0)
    for axis in "xy":
        for by in (1, 2, 3):
            if axis == "y" and by == 2:
                continue
            pl.semaphore_signal(barrier, inc=1, device_id=neighbour(axis, by), device_id_type=MESH)

    owner = d_ref[...] // 32
    pick = (lax.broadcasted_iota(jnp.int32, (32, 32), 0) == owner).astype(jnp.bfloat16)
    ordered = jnp.dot(pick, w_ref[...], preferred_element_type=jnp.float32).astype(jnp.bfloat16)
    source = lax.broadcasted_iota(jnp.int32, (512, 512), 0)
    target = lax.broadcasted_iota(jnp.int32, (512, 512), 1)
    apart = (source == target % 256 * 2 + target // 256).astype(jnp.bfloat16)
    ordered = jnp.dot(ordered, apart, preferred_element_type=jnp.float32)
    for k in range(4):
        send[:, k, :] = ordered[:, 128 * k : 128 * k + 128]
    pl.semaphore_wait(barrier, 36)

    def put(i, _):
        to = lax.rem(b + i, 32)
        pltpu.make_async_remote_copy(
            src_ref=send.at[to], dst_ref=land.at[b], send_sem=a_send, recv_sem=a_recv,
            device_id=(to, g), device_id_type=MESH,
        ).start()
        return 0

    lax.fori_loop(1, 32, put, 0)
    land[b] = send[b]
    every = pltpu.make_async_remote_copy(
        src_ref=send.at[pl.ds(0, 31)], dst_ref=land.at[pl.ds(0, 31)], send_sem=a_send, recv_sem=a_recv,
        device_id=sibling, device_id_type=MESH,
    )
    every.wait_recv()
    for k in range(4):
        held[yl, cx, k, yh, cz, core] = land[:, k, :].astype(jnp.bfloat16)

    pending, crossing, used = [], [], []

    def start(ref, to):
        index = len(used)
        used.append(index)
        copy = pltpu.make_async_remote_copy(
            src_ref=ref, dst_ref=ref, send_sem=s_sem.at[index], recv_sem=r_sem.at[index],
            device_id=to, device_id_type=MESH,
        )
        copy.start()
        pending.append(copy)
        return index

    def arrive(ref, index):
        pltpu.make_async_remote_copy(
            src_ref=ref, dst_ref=ref, send_sem=s_sem.at[index], recv_sem=r_sem.at[index],
            device_id=sibling, device_id_type=MESH,
        ).wait_recv()

    def across(**where):
        index = start(slot(core, **where), sibling)
        crossing.append((slot(1 - core, **where), index))

    def straight(axis, tiles, rows, **where):
        waits = []
        for by in (2, 1, 3) if axis != "z" else (4, 3, 5, 2, 6, 1, 7):
            index = start(slot(core, tiles, rows, **{**where, axis: here[axis]}), neighbour(axis, by))
            waits.append((slot(core, tiles, rows, **{**where, axis: shifted(axis, -by)}), index))
        return waits

    def settle(waits):
        for ref, index in waits:
            arrive(ref, index)

    first = pl.ds(0, 3)
    along_x = straight("x", 3, everywhere, y=here["y"], z=cz)
    along_z = straight("z", first, everywhere, x=cx, y=here["y"])
    settle(along_x)
    z_waits = straight("y", 3, everywhere, z=cz)
    settle(along_z)
    x_waits = straight("y", 0, everywhere, x=cx) + straight("y", 1, upper, x=cx)
    y_waits = straight("x", 2, everywhere, y=here["y"]) + straight("x", 1, lower, y=here["y"])

    own = {"x": [(0, upper), (0, lower), (1, upper)], "y": [(2, upper), (2, lower), (1, lower)], "z": [(3, upper), (3, lower)]}
    whole = {"x": [(0, everywhere), (1, upper)], "y": [(2, everywhere), (1, lower)], "z": [(3, everywhere)]}
    tickets = {}

    def launch(axis, piece, way, step, **part):
        tiles, rows = own[axis][piece]
        at = shifted(axis, -way * (step - 1))
        tickets[axis, piece, way, step] = start(slot(core, tiles, rows, **{axis: at}, **part), neighbour(axis, way))

    def landed(axis, piece, way, step, **part):
        tiles, rows = own[axis][piece]
        at = shifted(axis, -way * step)
        arrive(slot(core, tiles, rows, **{axis: at}, **part), tickets[axis, piece, way, step])

    def cross(axis, which, by):
        tiles, rows = whole[axis][which]
        across(tiles=tiles, rows=rows, **{axis: shifted(axis, by)})

    def begin(axis, waits):
        settle(waits)
        for piece in range(len(own[axis])):
            for way in (1, -1):
                launch(axis, piece, way, 1)
        for which in range(len(whole[axis])):
            cross(axis, which, 0)

    def z_round(piece, step):
        for way in (1, -1):
            landed("z", piece, way, step)
            if step < 3 or (way > 0) == (piece == 0):
                launch("z", piece, way, step + 1)

    def split(axis, way):
        if axis == "x":
            return {"y_low": 0 if way > 0 else 1}
        return {"x": pl.ds(0, 2) if way > 0 else pl.ds(2, 2)}

    def xy_round(axis, piece):
        for way in (1, -1):
            landed(axis, piece, way, 1)
            if piece == 2:
                launch(axis, piece, way, 2, **split(axis, way))
            elif (way > 0) == (piece == 0):
                launch(axis, piece, way, 2)

    begin("z", z_waits)
    begin("x", x_waits)
    begin("y", y_waits)
    z_round(0, 1)
    xy_round("x", 0)
    xy_round("y", 0)
    z_round(1, 1)
    cross("z", 0, 1)
    cross("z", 0, -1)
    z_round(0, 2)
    xy_round("x", 1)
    xy_round("y", 1)
    for axis in "xy":
        cross(axis, 0, 1)
        cross(axis, 0, -1)
    z_round(1, 2)
    cross("z", 0, 2)
    cross("z", 0, -2)
    z_round(0, 3)
    xy_round("x", 2)
    xy_round("y", 2)
    for axis in "xy":
        cross(axis, 1, 1)
        cross(axis, 1, -1)
    z_round(1, 3)
    cross("z", 0, 3)
    cross("z", 0, -3)
    for axis in "xy":
        landed(axis, 0, 1, 2)
        landed(axis, 1, -1, 2)
        cross(axis, 0, 2)
    landed("z", 0, 1, 4)
    landed("z", 1, -1, 4)
    cross("z", 0, 4)
    for axis in "xy":
        for way in (1, -1):
            landed(axis, 2, way, 2, **split(axis, way))
        cross(axis, 1, 2)
    for ref, index in crossing:
        arrive(ref, index)
    every.wait_send()
    for copy in pending:
        copy.wait_send()


def gather(waves, dest_of):
    count = 96
    return pl.pallas_call(
        gather_kernel,
        out_shape=pltpu.VMEM((2, 4, 4, 2, 8, 2, 32, 128), jnp.bfloat16),
        in_specs=[pl.BlockSpec(memory_space=pltpu.VMEM)] * 2,
        out_specs=pl.BlockSpec(memory_space=pltpu.VMEM),
        scratch_shapes=[
            pltpu.VMEM((32, 4, 128), jnp.float32),
            pltpu.VMEM((32, 4, 128), jnp.float32),
            pltpu.SemaphoreType.DMA,
            pltpu.SemaphoreType.DMA,
            pltpu.SemaphoreType.DMA((count,)),
            pltpu.SemaphoreType.DMA((count,)),
        ],
        compiler_params=pltpu.CompilerParams(
            collective_id=0, has_side_effects=True, vmem_limit_bytes=32 * 2**20
        ),
    )(waves, dest_of)


CONTRACT = (((1,), (1,)), ((), ()))


def correlate_kernel(g_ref, m_ref, o_ref, even_rows, odd_rows, sums, scale_ref, e_ref, stage, sem):
    blk, lag = lax.axis_index("blk"), lax.axis_index("lag")

    def shift():
        tile = pl.ds(pl.multiple_of(32 * blk, 32), 32)
        pick = lambda first: jnp.concatenate(
            [g_ref[4 * g + first + k, tile, :].astype(jnp.float32) for g in range(8) for k in (0, 1)], axis=1
        )
        even, odd = pick(0), pick(2)
        mean_square = jnp.sum(even * even + odd * odd, axis=1, keepdims=True) * (1.0 / 4096)
        factor = lax.rsqrt(mean_square + EPS)
        edge = jnp.zeros((32, 256), jnp.float32)
        extend = lambda x: jnp.concatenate(
            [edge, (x * factor).astype(jnp.bfloat16).astype(jnp.float32), edge], axis=1
        )
        even, odd = extend(even), extend(odd)
        by = 2304 + 32 * lag
        before = pltpu.roll(odd, by + 1, 1)[:, :2176]
        even, odd = pltpu.roll(even, by, 1)[:, :2176], pltpu.roll(odd, by, 1)[:, :2176]
        e_ref[0] = even
        e_ref[1] = odd - even
        e_ref[2] = before - even

    def build(chunk, rows_ref):
        for q in range(8):
            for kind in (1, 2, 0):
                x = jnp.broadcast_to(e_ref[kind, 8 * chunk + q : 8 * chunk + q + 1, :], (8, 2176))
                for half in range(2):
                    y = [pltpu.roll(x, 16 * half + 8 * e, 1, stride=1, stride_axis=0)[:, 128:] for e in (0, 1)]
                    at = 32 * q + 16 * half
                    rows_ref[kind, at : at + 16, :] = jnp.concatenate(y, 0).astype(jnp.bfloat16)

    def prepare(n):
        totals = []
        for r in range(4):
            rows = slice(256 * n + 64 * r, 256 * n + 64 * r + 64)
            total = jnp.zeros((64, 128), jnp.float32)
            for g in range(8):
                for lane in range(2):
                    v0 = g_ref[4 * g + lane, rows, :].astype(jnp.float32)
                    v1 = g_ref[4 * g + 2 + lane, rows, :].astype(jnp.float32)
                    sums[g, rows, 128 * lane : 128 * lane + 128] = (v0 + v1).astype(jnp.bfloat16)
                    total += v0 * v0 + v1 * v1
            totals.append(total)
        square = lax.dot_general(
            jnp.ones((8, 128), jnp.float32), jnp.concatenate(totals, 0), CONTRACT,
            precision=lax.Precision.HIGHEST, preferred_element_type=jnp.float32,
        )
        scale_ref[:, 256 * n : 256 * n + 256] = lax.rsqrt(square * (1.0 / 4096) + EPS) * (1.0 / 64)

    def columns(n, kind, g):
        rows = slice(256 * n, 256 * n + 256)
        if kind == 0:
            return sums[g, rows, :]
        first = 4 * g + (2 if kind == 1 else 0)
        return jnp.concatenate([g_ref[first, rows, :], g_ref[first + 1, rows, :]], axis=1)

    def away(chunk, tile):
        return pltpu.make_async_copy(
            stage.at[chunk % 2, tile],
            o_ref.at[pl.ds(8 * chunk, 8), :, pl.ds(128 * tile, 128)],
            sem.at[chunk % 2, tile],
        )

    def multiply(chunk, rows_ref):
        if chunk >= 2:
            for tile in range(8):
                away(chunk - 2, tile).wait()
        for n in range(4):
            if chunk == 0:
                prepare(n)
            products = {}
            for kind in (1, 2, 0):
                right = jnp.concatenate([columns(n, kind, g) for g in range(8)], axis=1)
                products[kind] = lax.dot_general(
                    rows_ref[kind], right, CONTRACT, preferred_element_type=jnp.float32
                )
            for c in range(2):
                cols = slice(256 * n + 128 * c, 256 * n + 128 * c + 128)
                lanes = slice(128 * c, 128 * c + 128)
                for q in range(8):
                    part = slice(32 * q, 32 * q + 32)
                    a = 8 * chunk + q
                    factor = m_ref[a : a + 1, cols].astype(jnp.float32) * scale_ref[0:1, cols]
                    for p in range(2):
                        value = (products[0][part, lanes] + products[1 + p][part, lanes]) * factor
                        stage[chunk % 2, 2 * n + c, q, pl.ds(p, 32, stride=2), :] = value
                away(chunk, 2 * n + c).start()

    shift()
    build(0, even_rows)
    for chunk in range(4):
        now, later = (even_rows, odd_rows) if chunk % 2 == 0 else (odd_rows, even_rows)
        if chunk < 3:
            build(chunk + 1, later)
        multiply(chunk, now)
    for chunk in (2, 3):
        for tile in range(8):
            away(chunk, tile).wait()


def correlate(everyone, pair_mask):
    return pl.pallas_call(
        correlate_kernel,
        out_shape=jax.ShapeDtypeStruct((32, 64, 1024), jnp.float32),
        in_specs=[pl.BlockSpec(memory_space=pltpu.VMEM)] * 2,
        out_specs=pl.BlockSpec(memory_space=pl.ANY),
        scratch_shapes=[
            pltpu.VMEM((3, 256, 2048), jnp.bfloat16),
            pltpu.VMEM((3, 256, 2048), jnp.bfloat16),
            pltpu.VMEM((8, 1024, 256), jnp.bfloat16),
            pltpu.VMEM((8, 1024), jnp.float32),
            pltpu.VMEM((3, 32, 2176), jnp.float32),
            pltpu.VMEM((2, 8, 8, 64, 128), jnp.float32),
            pltpu.SemaphoreType.DMA((2, 8)),
        ],
        compiler_params=pltpu.CompilerParams(vmem_limit_bytes=40 * 2**20),
    )(everyone, pair_mask)


def body(waves, dest_of, pair_mask):
    everyone = gather(waves, dest_of[None, :]).reshape(32, 1024, 128)
    return correlate(everyone, pair_mask)


def solution(mesh):
    in_specs = (P("blk", "lag"), P("blk"), P("blk", None))
    out_specs = P("blk", "lag", None)
    return jax.shard_map(body, mesh=mesh, in_specs=in_specs, out_specs=out_specs, check_vma=False)
```

```python
import functools

import jax
import jax.numpy as jnp
from jax import lax
from jax.sharding import PartitionSpec as P
import jax.experimental.pallas as pl
import jax.experimental.pallas.tpu as pltpu

EPS = 1e-06
LAGS = 512
MESH = pl.DeviceIdType.MESH
SIZES = {"x": 4, "y": 4, "z": 8}


def gather_kernel(w_hbm, d_hbm, held_x, held_y, held_z, w_ref, d_ref, in_sem, s_sem, r_sem):
    b, g = lax.axis_index("blk"), lax.axis_index("lag")
    core, cz, yh = b % 2, (b // 2) % 8, b // 16
    yl, cx = g // 4, g % 4
    cy = yh * 2 + yl
    here = {"x": cx, "y": cy, "z": cz}

    def device(pos, c):
        return ((pos["y"] // 2 * 8 + pos["z"]) * 2 + c, pos["y"] % 2 * 4 + pos["x"])

    def shifted(axis, by):
        n = SIZES[axis]
        return lax.rem(here[axis] + (by + n), n)

    def neighbour(axis, by):
        return device({**here, axis: shifted(axis, by)}, core)

    sibling = device(here, 1 - core)

    barrier = pltpu.get_barrier_semaphore()
    for axis in "xyz":
        for by in range(1, SIZES[axis]):
            pl.semaphore_signal(barrier, inc=1, device_id=neighbour(axis, by), device_id_type=MESH)
    pl.semaphore_signal(barrier, inc=1, device_id=sibling, device_id_type=MESH)

    fetch = [
        pltpu.make_async_copy(w_hbm, w_ref, in_sem.at[0]),
        pltpu.make_async_copy(d_hbm, d_ref, in_sem.at[1]),
    ]
    for copy in fetch:
        copy.start()
    source = lax.broadcasted_iota(jnp.int32, (512, 512), 0)
    target = lax.broadcasted_iota(jnp.int32, (1, 512), 1)
    apart = (source == target % 256 * 2 + target // 256).astype(jnp.bfloat16)
    to = lax.broadcasted_iota(jnp.int32, (256, 1), 0)
    of = lax.broadcasted_iota(jnp.int32, (1, 256), 1)
    place = lambda r: r // 16 % 8 * 2 + r // 128
    swap = ((place(to) == of % 16) & (to % 16 == place(of))).astype(jnp.bfloat16)
    for copy in fetch:
        copy.wait()
    owner = d_ref[...] // 32
    pick = (lax.broadcasted_iota(jnp.int32, (32, 32), 0) == owner).astype(jnp.bfloat16)
    ordered = jnp.dot(pick, w_ref[...], preferred_element_type=jnp.float32).astype(jnp.bfloat16)
    ordered = jnp.dot(ordered, apart, preferred_element_type=jnp.float32).astype(jnp.bfloat16)
    for k in range(3):
        held_x[core, cx, cy, cz, k] = ordered[:16, 128 * k : 128 * k + 128]
        held_y[core, cy, cx, cz, k] = ordered[16:, 128 * k : 128 * k + 128]
    for e in range(2):
        held_z[core, cz, cy, cx, e] = ordered[16 * e : 16 * e + 16, 384:]
    pl.semaphore_wait(barrier, 14)

    pending, used = {}, []

    def start(ref, to, unit):
        index = len(used)
        used.append(index)
        copy = pltpu.make_async_remote_copy(
            src_ref=ref, dst_ref=ref, send_sem=s_sem.at[index], recv_sem=r_sem.at[index],
            device_id=to, device_id_type=MESH,
        )
        copy.start()
        pending.setdefault(unit, []).append(copy)
        return index

    def arrive(ref, index):
        pltpu.make_async_remote_copy(
            src_ref=ref, dst_ref=ref, send_sem=s_sem.at[index], recv_sem=r_sem.at[index],
            device_id=sibling, device_id_type=MESH,
        ).wait_recv()

    def straight(unit, axis, ref_at):
        waits = {}
        for by in (2, 1, 3) if axis != "z" else (4, 3, 5, 2, 6, 1, 7):
            index = start(ref_at(here[axis]), neighbour(axis, by), (unit, 0))
            waits[by] = (ref_at(shifted(axis, -by)), index)
        return waits

    def settle(waits):
        for ref, index in waits.values():
            arrive(ref, index)

    crossing, tickets = {}, {}

    def piece_of(axis, at, piece):
        if axis == "x":
            return held_x.at[core, at, shifted("y", -piece)]
        if axis == "y":
            return held_y.at[core, at, shifted("x", -piece)]
        return held_z.at[core, at, pl.ds(2 * piece, 2)]

    def launch(axis, piece, way, step):
        at = shifted(axis, -way * (step - 1))
        unit = (axis, 0 if axis == "z" else -way * (step - 1))
        tickets[axis, piece, way, step] = start(piece_of(axis, at, piece), neighbour(axis, way), unit)

    def landed(axis, piece, way, step):
        arrive(piece_of(axis, shifted(axis, -way * step), piece), tickets[axis, piece, way, step])

    def begin(axis, piece):
        for way in (1, -1):
            launch(axis, piece, way, 1)

    def cross(axis, by):
        held = {"x": held_x, "y": held_y, "z": held_z}[axis]
        at = shifted(axis, by)
        index = start(held.at[core, at], sibling, (axis, 0 if axis == "z" else by))
        crossing[axis, by] = (held.at[1 - core, at], index)

    def z_round(piece, step):
        for way in (1, -1):
            landed("z", piece, way, step)
            if step < 3 or (way > 0) == (piece == 0):
                launch("z", piece, way, step + 1)

    forward = {0: 1, 1: -1, 2: 1, 3: -1}

    def xy_round(axis, piece):
        for way in (1, -1):
            landed(axis, piece, way, 1)
            if way == forward[piece]:
                launch(axis, piece, way, 2)

    def turn(views):
        joined = jnp.concatenate([ref[index].reshape(256, 128) for ref, index in views], axis=1)
        turned = jnp.dot(swap, joined, preferred_element_type=jnp.float32).astype(jnp.bfloat16)
        for k, (ref, index) in enumerate(views):
            ref[index] = turned[:, 128 * k : 128 * k + 128].reshape(2, 8, 16, 128)

    def ready(axis, bys):
        for by in bys:
            arrive(*crossing[axis, by])
        for by in bys if axis != "z" else (0,):
            for copy in pending.pop((axis, by)):
                copy.wait_send()

    def arrange(axis, by):
        ready(axis, (by,))
        held = held_x if axis == "x" else held_y
        at = shifted(axis, by)
        for part in range(2):
            turn([(held, (slice(None), at, 2 * part + near, slice(None), k)) for near in range(2) for k in range(3)])

    def arrange_z():
        ready("z", (0, 1, -1, 2, -2, 3, -3, 4))
        for y in range(4):
            turn([(held_z, (slice(None), slice(None), y, x, e)) for x in range(4) for e in range(2)])

    z_first = straight("z", "x", lambda at: held_z.at[core, cz, cy, at])
    x_first = straight("x", "z", lambda at: held_x.at[core, cx, cy, at])
    y_first = straight("y", "z", lambda at: held_y.at[core, cy, cx, at])
    settle(z_first)
    z_mid = straight("z", "y", lambda at: held_z.at[core, cz, at])
    settle(x_first)
    x_mid = straight("x", "y", lambda at: held_x.at[core, cx, at])
    begin("x", 0)
    settle(y_first)
    y_mid = straight("y", "x", lambda at: held_y.at[core, cy, at])
    begin("y", 0)
    settle(z_mid)
    begin("z", 0)
    begin("z", 1)
    cross("z", 0)
    for by in (1, 3, 2):
        arrive(*x_mid[by])
        begin("x", by)
    cross("x", 0)
    for by in (1, 3, 2):
        arrive(*y_mid[by])
        begin("y", by)
    cross("y", 0)
    z_round(0, 1)
    z_round(1, 1)
    cross("z", 1)
    cross("z", -1)
    xy_round("x", 0)
    xy_round("y", 0)
    z_round(0, 2)
    z_round(1, 2)
    cross("z", 2)
    cross("z", -2)
    xy_round("x", 1)
    xy_round("y", 1)
    z_round(0, 3)
    z_round(1, 3)
    cross("z", 3)
    cross("z", -3)
    xy_round("x", 3)
    xy_round("y", 3)
    xy_round("x", 2)
    cross("x", 1)
    cross("x", -1)
    xy_round("y", 2)
    cross("y", 1)
    cross("y", -1)
    arrange("x", 0)
    arrange("y", 0)
    landed("z", 0, 1, 4)
    landed("z", 1, -1, 4)
    cross("z", 4)
    for axis in "xy":
        arrange(axis, 1)
        arrange(axis, -1)
    for axis in "xy":
        for piece in (0, 1, 3, 2):
            landed(axis, piece, forward[piece], 2)
        cross(axis, 2)
    arrange_z()
    for axis in "xy":
        arrange(axis, 2)


def gather(waves, dest_of):
    count = 96
    return pl.pallas_call(
        gather_kernel,
        out_shape=[
            pltpu.VMEM((2, 4, 4, 8, 3, 16, 128), jnp.bfloat16),
            pltpu.VMEM((2, 4, 4, 8, 3, 16, 128), jnp.bfloat16),
            pltpu.VMEM((2, 8, 4, 4, 2, 16, 128), jnp.bfloat16),
        ],
        in_specs=[pl.BlockSpec(memory_space=pltpu.HBM)] * 2,
        out_specs=[pl.BlockSpec(memory_space=pltpu.VMEM)] * 3,
        scratch_shapes=[
            pltpu.VMEM((32, 512), jnp.bfloat16),
            pltpu.VMEM((1, 32), jnp.int32),
            pltpu.SemaphoreType.DMA((2,)),
            pltpu.SemaphoreType.DMA((count,)),
            pltpu.SemaphoreType.DMA((count,)),
        ],
        compiler_params=pltpu.CompilerParams(
            collective_id=0, has_side_effects=True, vmem_limit_bytes=16 * 2**20
        ),
    )(pltpu.with_memory_space_constraint(waves, pltpu.HBM), pltpu.with_memory_space_constraint(dest_of, pltpu.HBM))


CONTRACT = (((1,), (1,)), ((), ()))


def correlate_kernel(x_ref, y_ref, z_ref, m_hbm, o_ref, m_ref, m_sem, even_rows, odd_rows, sums, scale_ref, e_ref, stage, sem):
    blk, lag = lax.axis_index("blk"), lax.axis_index("lag")

    def shift():
        near, z, high = blk % 2, blk // 2 % 8, blk // 16

        def pick(first):
            lanes = []
            for g in range(8):
                for k in (first, first + 1):
                    x, rows = g % 4, []
                    for y in (g // 4, 2 + g // 4):
                        if k == 3:
                            rows.append(z_ref[near, z, y, x, high].astype(jnp.float32))
                        else:
                            a = x_ref[near, x, y, z, k].astype(jnp.float32)
                            b = y_ref[near, y, x, z, k].astype(jnp.float32)
                            rows.append(jnp.where(high == 0, a, b))
                    lanes.append(jnp.concatenate(rows, axis=0))
            return jnp.concatenate(lanes, axis=1)

        even, odd = pick(0), pick(2)
        mean_square = jnp.sum(even * even + odd * odd, axis=1, keepdims=True) * (1.0 / 4096)
        factor = lax.rsqrt(mean_square + EPS)
        edge = jnp.zeros((32, 256), jnp.float32)
        extend = lambda x: jnp.concatenate(
            [edge, (x * factor).astype(jnp.bfloat16).astype(jnp.float32), edge], axis=1
        )
        even, odd = extend(even), extend(odd)
        by = 2304 + 32 * lag
        before = pltpu.roll(odd, by + 1, 1)[:, :2176]
        even, odd = pltpu.roll(even, by, 1)[:, :2176], pltpu.roll(odd, by, 1)[:, :2176]
        e_ref[0] = even
        e_ref[1] = odd - even
        e_ref[2] = before - even

    def build(chunk, rows_ref):
        for q in range(8):
            for kind in (1, 2, 0):
                x = jnp.broadcast_to(e_ref[kind, 8 * chunk + q : 8 * chunk + q + 1, :], (8, 2176))
                for half in range(2):
                    y = [pltpu.roll(x, 16 * half + 8 * e, 1, stride=1, stride_axis=0)[:, 128:] for e in (0, 1)]
                    at = 32 * q + 16 * half
                    rows_ref[kind, at : at + 16, :] = jnp.concatenate(y, 0).astype(jnp.bfloat16)

    def records(q, high, g, k):
        e, near, z, y, x = q // 16, q % 2, q // 2 % 8, 2 * high + g // 4, g % 4
        if k == 3:
            return z_ref[near, z, y, x, e]
        return y_ref[near, y, x, z, k] if e else x_ref[near, x, y, z, k]

    def pieces(n):
        return [(q, high) for q in range(8 * n, 8 * n + 8) for high in (0, 1)]

    def prepare(n):
        totals = []
        for r, (q, high) in enumerate(pieces(n)):
            total = jnp.zeros((16, 128), jnp.float32)
            for g in range(8):
                for lane in range(2):
                    v0 = records(q, high, g, lane).astype(jnp.float32)
                    v1 = records(q, high, g, 2 + lane).astype(jnp.float32)
                    at = 256 * n + 16 * r
                    sums[g, at : at + 16, 128 * lane : 128 * lane + 128] = (v0 + v1).astype(jnp.bfloat16)
                    total += v0 * v0 + v1 * v1
            totals.append(total)
        square = lax.dot_general(
            jnp.ones((8, 128), jnp.float32), jnp.concatenate(totals, 0), CONTRACT,
            precision=lax.Precision.HIGHEST, preferred_element_type=jnp.float32,
        )
        scale_ref[:, 256 * n : 256 * n + 256] = lax.rsqrt(square * (1.0 / 4096) + EPS) * (1.0 / 64)

    def columns(n, kind, g):
        if kind == 0:
            return sums[g, 256 * n : 256 * n + 256, :]
        first = 2 if kind == 1 else 0
        return jnp.concatenate(
            [
                jnp.concatenate([records(q, high, g, first + k) for q, high in pieces(n)], axis=0)
                for k in (0, 1)
            ],
            axis=1,
        )

    def away(chunk, tile):
        return pltpu.make_async_copy(
            stage.at[chunk % 2, tile],
            o_ref.at[pl.ds(8 * chunk, 8), :, pl.ds(128 * tile, 128)],
            sem.at[chunk % 2, tile],
        )

    def multiply(chunk, rows_ref):
        if chunk >= 2:
            for tile in range(8):
                away(chunk - 2, tile).wait()
        for n in range(4):
            if chunk == 0:
                prepare(n)
            products = {}
            for kind in (1, 2, 0):
                right = jnp.concatenate([columns(n, kind, g) for g in range(8)], axis=1)
                products[kind] = lax.dot_general(
                    rows_ref[kind], right, CONTRACT, preferred_element_type=jnp.float32
                )
            for c in range(2):
                cols = slice(256 * n + 128 * c, 256 * n + 128 * c + 128)
                lanes = slice(128 * c, 128 * c + 128)
                for q in range(8):
                    part = slice(32 * q, 32 * q + 32)
                    a = 8 * chunk + q
                    factor = m_ref[a : a + 1, cols].astype(jnp.float32) * scale_ref[0:1, cols]
                    for p in range(2):
                        value = (products[0][part, lanes] + products[1 + p][part, lanes]) * factor
                        stage[chunk % 2, 2 * n + c, q, pl.ds(p, 32, stride=2), :] = value
                away(chunk, 2 * n + c).start()

    fetch = pltpu.make_async_copy(m_hbm, m_ref, m_sem)
    fetch.start()
    shift()
    build(0, even_rows)
    fetch.wait()
    for chunk in range(4):
        now, later = (even_rows, odd_rows) if chunk % 2 == 0 else (odd_rows, even_rows)
        if chunk < 3:
            build(chunk + 1, later)
        multiply(chunk, now)
    for chunk in (2, 3):
        for tile in range(8):
            away(chunk, tile).wait()


def correlate(everyone_x, everyone_y, everyone_z, pair_mask):
    return pl.pallas_call(
        correlate_kernel,
        out_shape=jax.ShapeDtypeStruct((32, 64, 1024), jnp.float32),
        in_specs=[pl.BlockSpec(memory_space=pltpu.VMEM)] * 3 + [pl.BlockSpec(memory_space=pltpu.HBM)],
        out_specs=pl.BlockSpec(memory_space=pl.ANY),
        scratch_shapes=[
            pltpu.VMEM((32, 1024), jnp.int32),
            pltpu.SemaphoreType.DMA,
            pltpu.VMEM((3, 256, 2048), jnp.bfloat16),
            pltpu.VMEM((3, 256, 2048), jnp.bfloat16),
            pltpu.VMEM((8, 1024, 256), jnp.bfloat16),
            pltpu.VMEM((8, 1024), jnp.float32),
            pltpu.VMEM((3, 32, 2176), jnp.float32),
            pltpu.VMEM((2, 8, 8, 64, 128), jnp.float32),
            pltpu.SemaphoreType.DMA((2, 8)),
        ],
        compiler_params=pltpu.CompilerParams(vmem_limit_bytes=40 * 2**20),
    )(everyone_x, everyone_y, everyone_z, pltpu.with_memory_space_constraint(pair_mask, pltpu.HBM))


def body(waves, dest_of, pair_mask):
    return correlate(*gather(waves, dest_of[None, :]), pair_mask)


def solution(mesh):
    in_specs = (P("blk", "lag"), P("blk"), P("blk", None))
    out_specs = P("blk", "lag", None)
    return jax.shard_map(body, mesh=mesh, in_specs=in_specs, out_specs=out_specs, check_vma=False)
```

```python
import functools

import jax
import jax.numpy as jnp
from jax import lax
from jax.sharding import PartitionSpec as P
import jax.experimental.pallas as pl
import jax.experimental.pallas.tpu as pltpu

EPS = 1e-06
LAGS = 512
MESH = pl.DeviceIdType.MESH
SIZES = {"x": 4, "y": 4, "z": 8}


def gather_kernel(
    w_hbm, d_hbm, held_x, held_y, held_z, sum_x, sum_y, squares, w_ref, d_ref, in_sem, s_sem, r_sem
):
    b, g = lax.axis_index("blk"), lax.axis_index("lag")
    core, cz, yh = b % 2, (b // 2) % 8, b // 16
    yl, cx = g // 4, g % 4
    cy = yh * 2 + yl
    here = {"x": cx, "y": cy, "z": cz}

    def device(pos, c):
        return ((pos["y"] // 2 * 8 + pos["z"]) * 2 + c, pos["y"] % 2 * 4 + pos["x"])

    def shifted(axis, by):
        n = SIZES[axis]
        return lax.rem(here[axis] + (by + n), n)

    def neighbour(axis, by):
        return device({**here, axis: shifted(axis, by)}, core)

    sibling = device(here, 1 - core)

    barrier = pltpu.get_barrier_semaphore()
    for axis in "xyz":
        for by in range(1, SIZES[axis]):
            pl.semaphore_signal(barrier, inc=1, device_id=neighbour(axis, by), device_id_type=MESH)
    pl.semaphore_signal(barrier, inc=1, device_id=sibling, device_id_type=MESH)

    fetch = [
        pltpu.make_async_copy(w_hbm, w_ref, in_sem.at[0]),
        pltpu.make_async_copy(d_hbm, d_ref, in_sem.at[1]),
    ]
    for copy in fetch:
        copy.start()
    squares[...] = jnp.zeros_like(squares)
    source = lax.broadcasted_iota(jnp.int32, (512, 512), 0)
    target = lax.broadcasted_iota(jnp.int32, (1, 512), 1)
    apart = (source == target % 256 * 2 + target // 256).astype(jnp.bfloat16)
    to = lax.broadcasted_iota(jnp.int32, (256, 1), 0)
    of = lax.broadcasted_iota(jnp.int32, (1, 256), 1)
    place = lambda r: r // 16 % 8 * 2 + r // 128
    swap = ((place(to) == of % 16) & (to % 16 == place(of))).astype(jnp.bfloat16)
    for copy in fetch:
        copy.wait()
    owner = d_ref[...] // 32
    pick = (lax.broadcasted_iota(jnp.int32, (32, 32), 0) == owner).astype(jnp.bfloat16)
    ordered = jnp.dot(pick, w_ref[...], preferred_element_type=jnp.float32).astype(jnp.bfloat16)
    ordered = jnp.dot(ordered, apart, preferred_element_type=jnp.float32).astype(jnp.bfloat16)
    for k in range(3):
        held_x[core, cx, cy, cz, k] = ordered[:16, 128 * k : 128 * k + 128]
        held_y[core, cy, cx, cz, k] = ordered[16:, 128 * k : 128 * k + 128]
    for e in range(2):
        held_z[core, cz, cy, cx, e] = ordered[16 * e : 16 * e + 16, 384:]
    pl.semaphore_wait(barrier, 14)

    pending, used = {}, []

    def start(ref, to, unit):
        index = len(used)
        used.append(index)
        copy = pltpu.make_async_remote_copy(
            src_ref=ref, dst_ref=ref, send_sem=s_sem.at[index], recv_sem=r_sem.at[index],
            device_id=to, device_id_type=MESH,
        )
        copy.start()
        pending.setdefault(unit, []).append(copy)
        return index

    def arrive(ref, index):
        pltpu.make_async_remote_copy(
            src_ref=ref, dst_ref=ref, send_sem=s_sem.at[index], recv_sem=r_sem.at[index],
            device_id=sibling, device_id_type=MESH,
        ).wait_recv()

    def straight(unit, axis, ref_at, places=(2, 1, 3)):
        waits = {}
        for by in places:
            index = start(ref_at(here[axis]), neighbour(axis, by), (unit, 0))
            waits[by] = (ref_at(shifted(axis, -by)), index)
        return waits

    def settle(waits):
        for ref, index in waits.values():
            arrive(ref, index)

    crossing, tickets = {}, {}

    def piece_of(axis, at, piece):
        if axis == "x":
            return held_x.at[core, at, shifted("y", -piece)]
        if axis == "y":
            return held_y.at[core, at, shifted("x", -piece)]
        return held_z.at[core, at, pl.ds(2 * piece, 2)]

    def launch(axis, piece, way, step):
        at = shifted(axis, -way * (step - 1))
        unit = (axis, 0 if axis == "z" else -way * (step - 1))
        tickets[axis, piece, way, step] = start(piece_of(axis, at, piece), neighbour(axis, way), unit)

    def landed(axis, piece, way, step):
        arrive(piece_of(axis, shifted(axis, -way * step), piece), tickets[axis, piece, way, step])

    def begin(axis, piece):
        for way in (1, -1):
            launch(axis, piece, way, 1)

    def cross(axis, by):
        held = {"x": held_x, "y": held_y, "z": held_z}[axis]
        at = shifted(axis, by)
        index = start(held.at[core, at], sibling, (axis, 0 if axis == "z" else by))
        crossing[axis, by] = (held.at[1 - core, at], index)

    def z_round(piece, step):
        for way in (1, -1):
            landed("z", piece, way, step)
            if step < 3 or (way > 0) == (piece == 0):
                launch("z", piece, way, step + 1)

    forward = {0: 1, 1: -1, 2: 1, 3: -1}

    def xy_round(axis, piece):
        for way in (1, -1):
            landed(axis, piece, way, 1)
            if way == forward[piece]:
                launch(axis, piece, way, 2)

    def pass_on(axis, other, held, at, waits):
        far = {}
        for by, way, half in ((1, 1, pl.ds(0, 4)), (3, -1, pl.ds(4, 4))):
            arrive(*waits[by])
            index = start(held.at[core, at, shifted(other, -way), half], neighbour(other, way), (axis, 0))
            far[by] = (held.at[core, at, shifted(other, 2), half], index)
            begin(axis, by)
        return far

    def turn(views):
        joined = jnp.concatenate([ref[index].reshape(256, 128) for ref, index in views], axis=1)
        turned = jnp.dot(swap, joined, preferred_element_type=jnp.float32)
        values = [turned[:, 128 * k : 128 * k + 128] for k in range(len(views))]
        for value, (ref, index) in zip(values, views):
            ref[index] = value.astype(jnp.bfloat16).reshape(2, 8, 16, 128)
        return values

    def turn_lines(axis, at, lines):
        held, sums, e = (held_x, sum_x, 0) if axis == "x" else (held_y, sum_y, 1)
        values = turn([(held, (slice(None), at, line, slice(None), k)) for line in lines for k in range(3)])
        for n, line in enumerate(lines):
            a, b, c = values[3 * n : 3 * n + 3]
            sums[:, at, line, :, 0] = (a + c).astype(jnp.bfloat16).reshape(2, 8, 16, 128)
            high = (line if axis == "x" else at) // 2
            squares[e, high] += a * a + b * b + c * c

    def ready(axis, bys):
        for by in bys:
            arrive(*crossing[axis, by])
        for by in bys if axis != "z" else (0,):
            for copy in pending.pop((axis, by)):
                copy.wait_send()

    def arrange(axis, by):
        ready(axis, (by,))
        at = shifted(axis, by)
        for part in range(2):
            turn_lines(axis, at, (2 * part, 2 * part + 1))

    def last_line(axis, piece):
        held, other = (held_x, "y") if axis == "x" else (held_y, "x")
        return held, shifted(axis, 2), shifted(other, -piece)

    def last_landed(axis, piece):
        landed(axis, piece, forward[piece], 2)
        held, at, line = last_line(axis, piece)
        index = start(held.at[core, at, line], sibling, (axis, 4 + piece))
        crossing[axis, 4 + piece] = (held.at[1 - core, at, line], index)

    def last_arrange(axis, piece):
        ready(axis, (4 + piece,))
        held, at, line = last_line(axis, piece)
        turn_lines(axis, at, (line,))

    def arrange_z():
        ready("z", (0, 1, -1, 2, -2, 3, -3, 4))
        for y in range(4):
            views = [(held_z, (slice(None), slice(None), y, x, e)) for e in range(2) for x in range(4)]
            values = turn(views)
            for e in range(2):
                a, b, c, d = values[4 * e : 4 * e + 4]
                squares[e, y // 2] += a * a + b * b + c * c + d * d

    def second_sums():
        for y in range(4):
            for x in range(4):
                for sums, held, place, e in ((sum_x, held_x, (x, y), 0), (sum_y, held_y, (y, x), 1)):
                    near = held[:, place[0], place[1], :, 1].astype(jnp.float32)
                    far = held_z[:, :, y, x, e].astype(jnp.float32)
                    sums[:, place[0], place[1], :, 1] = (near + far).astype(jnp.bfloat16)

    z_first = straight("z", "x", lambda at: held_z.at[core, cz, cy, at])
    x_first = straight("x", "z", lambda at: held_x.at[core, cx, cy, at], (4, 3, 5, 2, 6, 1, 7))
    y_first = straight("y", "z", lambda at: held_y.at[core, cy, cx, at], (4, 3, 5, 2, 6, 1, 7))
    settle(z_first)
    z_mid = straight("z", "y", lambda at: held_z.at[core, cz, at])
    settle(x_first)
    x_mid = straight("x", "y", lambda at: held_x.at[core, cx, at], (1, 3))
    begin("x", 0)
    settle(y_first)
    y_mid = straight("y", "x", lambda at: held_y.at[core, cy, at], (1, 3))
    begin("y", 0)
    settle(z_mid)
    begin("z", 0)
    begin("z", 1)
    cross("z", 0)
    far_x = pass_on("x", "y", held_x, cx, x_mid)
    far_y = pass_on("y", "x", held_y, cy, y_mid)
    z_round(0, 1)
    z_round(1, 1)
    cross("z", 1)
    cross("z", -1)
    xy_round("x", 0)
    xy_round("y", 0)
    settle(far_x)
    begin("x", 2)
    cross("x", 0)
    settle(far_y)
    begin("y", 2)
    cross("y", 0)
    z_round(0, 2)
    z_round(1, 2)
    cross("z", 2)
    cross("z", -2)
    xy_round("x", 1)
    xy_round("y", 1)
    z_round(0, 3)
    z_round(1, 3)
    cross("z", 3)
    cross("z", -3)
    xy_round("x", 3)
    xy_round("y", 3)
    xy_round("x", 2)
    cross("x", 1)
    cross("x", -1)
    xy_round("y", 2)
    cross("y", 1)
    cross("y", -1)
    arrange("x", 0)
    arrange("y", 0)
    for piece in (0, 1):
        for axis in "xy":
            last_landed(axis, piece)
    landed("z", 0, 1, 4)
    landed("z", 1, -1, 4)
    cross("z", 4)
    for axis in "xy":
        arrange(axis, 1)
        arrange(axis, -1)
    for axis in "xy":
        last_landed(axis, 3)
    for piece in (0, 1):
        for axis in "xy":
            last_arrange(axis, piece)
    for axis in "xy":
        last_landed(axis, 2)
    arrange_z()
    for piece in (3, 2):
        for axis in "xy":
            last_arrange(axis, piece)
    second_sums()


def gather(waves, dest_of):
    count = 96
    return pl.pallas_call(
        gather_kernel,
        out_shape=[
            pltpu.VMEM((2, 4, 4, 8, 3, 16, 128), jnp.bfloat16),
            pltpu.VMEM((2, 4, 4, 8, 3, 16, 128), jnp.bfloat16),
            pltpu.VMEM((2, 8, 4, 4, 2, 16, 128), jnp.bfloat16),
            pltpu.VMEM((2, 4, 4, 8, 2, 16, 128), jnp.bfloat16),
            pltpu.VMEM((2, 4, 4, 8, 2, 16, 128), jnp.bfloat16),
            pltpu.VMEM((2, 2, 256, 128), jnp.float32),
        ],
        in_specs=[pl.BlockSpec(memory_space=pltpu.HBM)] * 2,
        out_specs=[pl.BlockSpec(memory_space=pltpu.VMEM)] * 6,
        scratch_shapes=[
            pltpu.VMEM((32, 512), jnp.bfloat16),
            pltpu.VMEM((1, 32), jnp.int32),
            pltpu.SemaphoreType.DMA((2,)),
            pltpu.SemaphoreType.DMA((count,)),
            pltpu.SemaphoreType.DMA((count,)),
        ],
        compiler_params=pltpu.CompilerParams(
            collective_id=0, has_side_effects=True, vmem_limit_bytes=24 * 2**20
        ),
    )(pltpu.with_memory_space_constraint(waves, pltpu.HBM), pltpu.with_memory_space_constraint(dest_of, pltpu.HBM))


CONTRACT = (((1,), (1,)), ((), ()))


def correlate_kernel(
    x_ref, y_ref, z_ref, sum_x, sum_y, squares, m_hbm, o_ref,
    m_ref, m_sem, even_rows, odd_rows, scale_ref, e_ref, stage, sem,
):
    blk, lag = lax.axis_index("blk"), lax.axis_index("lag")

    def shift():
        near, z, high = blk % 2, blk // 2 % 8, blk // 16

        def pick(first):
            lanes = []
            for g in range(8):
                for k in (first, first + 1):
                    x, rows = g % 4, []
                    for y in (g // 4, 2 + g // 4):
                        if k == 3:
                            rows.append(z_ref[near, z, y, x, high].astype(jnp.float32))
                        else:
                            a = x_ref[near, x, y, z, k].astype(jnp.float32)
                            b = y_ref[near, y, x, z, k].astype(jnp.float32)
                            rows.append(jnp.where(high == 0, a, b))
                    lanes.append(jnp.concatenate(rows, axis=0))
            return jnp.concatenate(lanes, axis=1)

        even, odd = pick(0), pick(2)
        mean_square = jnp.sum(even * even + odd * odd, axis=1, keepdims=True) * (1.0 / 4096)
        factor = lax.rsqrt(mean_square + EPS)
        edge = jnp.zeros((32, 256), jnp.float32)
        extend = lambda x: jnp.concatenate(
            [edge, (x * factor).astype(jnp.bfloat16).astype(jnp.float32), edge], axis=1
        )
        even, odd = extend(even), extend(odd)
        by = 2304 + 32 * lag
        before = pltpu.roll(odd, by + 1, 1)[:, :2176]
        even, odd = pltpu.roll(even, by, 1)[:, :2176], pltpu.roll(odd, by, 1)[:, :2176]
        e_ref[0] = even
        e_ref[1] = odd - even
        e_ref[2] = before - even

    def build(chunk, rows_ref):
        for q in range(8):
            for kind in (1, 2, 0):
                x = jnp.broadcast_to(e_ref[kind, 8 * chunk + q : 8 * chunk + q + 1, :], (8, 2176))
                for half in range(2):
                    y = [pltpu.roll(x, 16 * half + 8 * e, 1, stride=1, stride_axis=0)[:, 128:] for e in (0, 1)]
                    at = 32 * q + 16 * half
                    rows_ref[kind, at : at + 16, :] = jnp.concatenate(y, 0).astype(jnp.bfloat16)

    def records(q, high, g, k):
        e, near, z, y, x = q // 16, q % 2, q // 2 % 8, 2 * high + g // 4, g % 4
        if k >= 4:
            return sum_y[near, y, x, z, k - 4] if e else sum_x[near, x, y, z, k - 4]
        if k == 3:
            return z_ref[near, z, y, x, e]
        return y_ref[near, y, x, z, k] if e else x_ref[near, x, y, z, k]

    def pieces(n):
        return [(q, high) for q in range(8 * n, 8 * n + 8) for high in (0, 1)]

    def prepare(n):
        totals = []
        for q, high in pieces(n):
            at = 16 * (q % 2 * 8 + q // 2 % 8)
            totals.append(squares[q // 16, high, at : at + 16, :])
        square = lax.dot_general(
            jnp.ones((8, 128), jnp.float32), jnp.concatenate(totals, 0), CONTRACT,
            precision=lax.Precision.HIGHEST, preferred_element_type=jnp.float32,
        )
        scale_ref[:, 256 * n : 256 * n + 256] = lax.rsqrt(square * (1.0 / 4096) + EPS) * (1.0 / 64)

    def columns(n, kind, g):
        first = (4, 2, 0)[kind]
        return jnp.concatenate(
            [
                jnp.concatenate([records(q, high, g, first + k) for q, high in pieces(n)], axis=0)
                for k in (0, 1)
            ],
            axis=1,
        )

    def away(chunk, tile):
        return pltpu.make_async_copy(
            stage.at[chunk % 2, tile],
            o_ref.at[pl.ds(8 * chunk, 8), :, pl.ds(128 * tile, 128)],
            sem.at[chunk % 2, tile],
        )

    def multiply(chunk, rows_ref):
        if chunk >= 2:
            for tile in range(8):
                away(chunk - 2, tile).wait()
        for n in range(4):
            if chunk == 0:
                prepare(n)
            products = {}
            for kind in (1, 2, 0):
                right = jnp.concatenate([columns(n, kind, g) for g in range(8)], axis=1)
                products[kind] = lax.dot_general(
                    rows_ref[kind], right, CONTRACT, preferred_element_type=jnp.float32
                )
            for c in range(2):
                cols = slice(256 * n + 128 * c, 256 * n + 128 * c + 128)
                lanes = slice(128 * c, 128 * c + 128)
                for q in range(8):
                    part = slice(32 * q, 32 * q + 32)
                    a = 8 * chunk + q
                    factor = m_ref[a : a + 1, cols].astype(jnp.float32) * scale_ref[0:1, cols]
                    for p in range(2):
                        value = (products[0][part, lanes] + products[1 + p][part, lanes]) * factor
                        stage[chunk % 2, 2 * n + c, q, pl.ds(p, 32, stride=2), :] = value
                away(chunk, 2 * n + c).start()

    fetch = pltpu.make_async_copy(m_hbm, m_ref, m_sem)
    fetch.start()
    shift()
    build(0, even_rows)
    fetch.wait()
    for chunk in range(4):
        now, later = (even_rows, odd_rows) if chunk % 2 == 0 else (odd_rows, even_rows)
        if chunk < 3:
            build(chunk + 1, later)
        multiply(chunk, now)
    for chunk in (2, 3):
        for tile in range(8):
            away(chunk, tile).wait()


def correlate(gathered, pair_mask):
    return pl.pallas_call(
        correlate_kernel,
        out_shape=jax.ShapeDtypeStruct((32, 64, 1024), jnp.float32),
        in_specs=[pl.BlockSpec(memory_space=pltpu.VMEM)] * 6 + [pl.BlockSpec(memory_space=pltpu.HBM)],
        out_specs=pl.BlockSpec(memory_space=pl.ANY),
        scratch_shapes=[
            pltpu.VMEM((32, 1024), jnp.int32),
            pltpu.SemaphoreType.DMA,
            pltpu.VMEM((3, 256, 2048), jnp.bfloat16),
            pltpu.VMEM((3, 256, 2048), jnp.bfloat16),
            pltpu.VMEM((8, 1024), jnp.float32),
            pltpu.VMEM((3, 32, 2176), jnp.float32),
            pltpu.VMEM((2, 8, 8, 64, 128), jnp.float32),
            pltpu.SemaphoreType.DMA((2, 8)),
        ],
        compiler_params=pltpu.CompilerParams(vmem_limit_bytes=40 * 2**20),
    )(*gathered, pltpu.with_memory_space_constraint(pair_mask, pltpu.HBM))


def body(waves, dest_of, pair_mask):
    return correlate(gather(waves, dest_of[None, :]), pair_mask)


def solution(mesh):
    in_specs = (P("blk", "lag"), P("blk"), P("blk", None))
    out_specs = P("blk", "lag", None)
    return jax.shard_map(body, mesh=mesh, in_specs=in_specs, out_specs=out_specs, check_vma=False)
```

```python
import functools

import jax
import jax.numpy as jnp
from jax import lax
from jax.sharding import PartitionSpec as P
import jax.experimental.pallas as pl
import jax.experimental.pallas.tpu as pltpu

EPS = 1e-06
LAGS = 512
MESH = pl.DeviceIdType.MESH
SIZES = {"x": 4, "y": 4, "z": 8}


def gather_kernel(
    w_hbm, d_hbm, held_x, held_y, held_z, sum_x, sum_y, squares, w_ref, d_ref, in_sem, s_sem, r_sem
):
    b, g = lax.axis_index("blk"), lax.axis_index("lag")
    core, cz, yh = b % 2, (b // 2) % 8, b // 16
    yl, cx = g // 4, g % 4
    cy = yh * 2 + yl
    here = {"x": cx, "y": cy, "z": cz}

    def device(pos, c):
        return ((pos["y"] // 2 * 8 + pos["z"]) * 2 + c, pos["y"] % 2 * 4 + pos["x"])

    def shifted(axis, by):
        n = SIZES[axis]
        return lax.rem(here[axis] + (by + n), n)

    def neighbour(axis, by):
        return device({**here, axis: shifted(axis, by)}, core)

    sibling = device(here, 1 - core)

    barrier = pltpu.get_barrier_semaphore()
    for axis in "xyz":
        for by in range(1, SIZES[axis]):
            pl.semaphore_signal(barrier, inc=1, device_id=neighbour(axis, by), device_id_type=MESH)
    pl.semaphore_signal(barrier, inc=1, device_id=sibling, device_id_type=MESH)

    fetch = [
        pltpu.make_async_copy(w_hbm, w_ref, in_sem.at[0]),
        pltpu.make_async_copy(d_hbm, d_ref, in_sem.at[1]),
    ]
    for copy in fetch:
        copy.start()
    squares[...] = jnp.zeros_like(squares)
    source = lax.broadcasted_iota(jnp.int32, (512, 512), 0)
    target = lax.broadcasted_iota(jnp.int32, (1, 512), 1)
    apart = (source == target % 256 * 2 + target // 256).astype(jnp.bfloat16)
    to = lax.broadcasted_iota(jnp.int32, (256, 1), 0)
    of = lax.broadcasted_iota(jnp.int32, (1, 256), 1)
    place = lambda r: r // 16 % 8 * 2 + r // 128
    swap = ((place(to) == of % 16) & (to % 16 == place(of))).astype(jnp.bfloat16)
    for copy in fetch:
        copy.wait()
    owner = d_ref[...] // 32
    pick = (lax.broadcasted_iota(jnp.int32, (32, 32), 0) == owner).astype(jnp.bfloat16)
    ordered = jnp.dot(pick, w_ref[...], preferred_element_type=jnp.float32).astype(jnp.bfloat16)
    ordered = jnp.dot(ordered, apart, preferred_element_type=jnp.float32).astype(jnp.bfloat16)
    for k in range(3):
        held_x[core, cx, cy, cz, k] = ordered[:16, 128 * k : 128 * k + 128]
        held_y[core, cy, cx, cz, k] = ordered[16:, 128 * k : 128 * k + 128]
    for e in range(2):
        held_z[core, cz, cy, cx, e] = ordered[16 * e : 16 * e + 16, 384:]
    pl.semaphore_wait(barrier, 14)

    pending, used = {}, []

    def start(ref, to, unit):
        index = len(used)
        used.append(index)
        copy = pltpu.make_async_remote_copy(
            src_ref=ref, dst_ref=ref, send_sem=s_sem.at[index], recv_sem=r_sem.at[index],
            device_id=to, device_id_type=MESH,
        )
        copy.start()
        pending.setdefault(unit, []).append(copy)
        return index

    def arrive(ref, index):
        pltpu.make_async_remote_copy(
            src_ref=ref, dst_ref=ref, send_sem=s_sem.at[index], recv_sem=r_sem.at[index],
            device_id=sibling, device_id_type=MESH,
        ).wait_recv()

    def straight(unit, axis, ref_at, places=(2, 1, 3)):
        waits = {}
        for by in places:
            index = start(ref_at(here[axis]), neighbour(axis, by), (unit, 0))
            waits[by] = (ref_at(shifted(axis, -by)), index)
        return waits

    def settle(waits):
        for ref, index in waits.values():
            arrive(ref, index)

    crossing, tickets = {}, {}

    def piece_of(axis, at, piece):
        if axis == "x":
            return held_x.at[core, at, shifted("y", -piece)]
        if axis == "y":
            return held_y.at[core, at, shifted("x", -piece)]
        return held_z.at[core, at, pl.ds(2 * piece, 2)]

    def launch(axis, piece, way, step):
        at = shifted(axis, -way * (step - 1))
        unit = (axis, 0 if axis == "z" else -way * (step - 1))
        tickets[axis, piece, way, step] = start(piece_of(axis, at, piece), neighbour(axis, way), unit)

    def landed(axis, piece, way, step):
        arrive(piece_of(axis, shifted(axis, -way * step), piece), tickets[axis, piece, way, step])

    def begin(axis, piece):
        for way in (1, -1):
            launch(axis, piece, way, 1)

    def cross(axis, by):
        held = {"x": held_x, "y": held_y, "z": held_z}[axis]
        at = shifted(axis, by)
        index = start(held.at[core, at], sibling, (axis, 0 if axis == "z" else by))
        crossing[axis, by] = (held.at[1 - core, at], index)

    def z_round(piece, step):
        for way in (1, -1):
            landed("z", piece, way, step)
            if step < 3 or (way > 0) == (piece == 0):
                launch("z", piece, way, step + 1)

    forward = {0: 1, 1: -1, 2: 1, 3: -1}

    def xy_round(axis, piece):
        for way in (1, -1):
            landed(axis, piece, way, 1)
            if way == forward[piece]:
                launch(axis, piece, way, 2)

    def pass_on(axis, waits):
        for by in (1, 3):
            arrive(*waits[by])
            begin(axis, by)
        return {2: waits[2]}

    def turn(views):
        joined = jnp.concatenate([ref[index].reshape(256, 128) for ref, index in views], axis=1)
        turned = jnp.dot(swap, joined, preferred_element_type=jnp.float32)
        values = [turned[:, 128 * k : 128 * k + 128] for k in range(len(views))]
        for value, (ref, index) in zip(values, views):
            ref[index] = value.astype(jnp.bfloat16).reshape(2, 8, 16, 128)
        return values

    def turn_lines(axis, at, lines):
        held, sums, e = (held_x, sum_x, 0) if axis == "x" else (held_y, sum_y, 1)
        values = turn([(held, (slice(None), at, line, slice(None), k)) for line in lines for k in range(3)])
        for n, line in enumerate(lines):
            a, b, c = values[3 * n : 3 * n + 3]
            sums[:, at, line, :, 0] = (a + c).astype(jnp.bfloat16).reshape(2, 8, 16, 128)
            high = (line if axis == "x" else at) // 2
            squares[e, high] += a * a + b * b + c * c

    def ready(axis, bys):
        for by in bys:
            arrive(*crossing[axis, by])
        for by in bys if axis != "z" else (0,):
            for copy in pending.pop((axis, by)):
                copy.wait_send()

    def arrange(axis, by):
        ready(axis, (by,))
        at = shifted(axis, by)
        for part in range(2):
            turn_lines(axis, at, (2 * part, 2 * part + 1))

    def last_line(axis, piece):
        held, other = (held_x, "y") if axis == "x" else (held_y, "x")
        return held, shifted(axis, 2), shifted(other, -piece)

    def last_landed(axis, piece):
        landed(axis, piece, forward[piece], 2)
        held, at, line = last_line(axis, piece)
        index = start(held.at[core, at, line], sibling, (axis, 4 + piece))
        crossing[axis, 4 + piece] = (held.at[1 - core, at, line], index)

    def last_arrange(axis, piece):
        ready(axis, (4 + piece,))
        held, at, line = last_line(axis, piece)
        turn_lines(axis, at, (line,))

    def arrange_z():
        ready("z", (0, 1, -1, 2, -2, 3, -3, 4))
        for y in range(4):
            views = [(held_z, (slice(None), slice(None), y, x, e)) for e in range(2) for x in range(4)]
            values = turn(views)
            for e in range(2):
                a, b, c, d = values[4 * e : 4 * e + 4]
                squares[e, y // 2] += a * a + b * b + c * c + d * d

    def second_sums():
        for y in range(4):
            for x in range(4):
                for sums, held, place, e in ((sum_x, held_x, (x, y), 0), (sum_y, held_y, (y, x), 1)):
                    near = held[:, place[0], place[1], :, 1].astype(jnp.float32)
                    far = held_z[:, :, y, x, e].astype(jnp.float32)
                    sums[:, place[0], place[1], :, 1] = (near + far).astype(jnp.bfloat16)

    z_first = straight("z", "x", lambda at: held_z.at[core, cz, cy, at])
    x_first = straight("x", "z", lambda at: held_x.at[core, cx, cy, at], (4, 3, 5, 2, 6, 1, 7))
    y_first = straight("y", "z", lambda at: held_y.at[core, cy, cx, at], (4, 3, 5, 2, 6, 1, 7))
    settle(z_first)
    z_mid = straight("z", "y", lambda at: held_z.at[core, cz, at])
    settle(x_first)
    x_mid = straight("x", "y", lambda at: held_x.at[core, cx, at])
    begin("x", 0)
    settle(y_first)
    y_mid = straight("y", "x", lambda at: held_y.at[core, cy, at])
    begin("y", 0)
    settle(z_mid)
    begin("z", 0)
    begin("z", 1)
    cross("z", 0)
    far_x = pass_on("x", x_mid)
    far_y = pass_on("y", y_mid)
    xy_round("x", 0)
    xy_round("y", 0)
    z_round(0, 1)
    z_round(1, 1)
    cross("z", 1)
    cross("z", -1)
    settle(far_x)
    begin("x", 2)
    cross("x", 0)
    settle(far_y)
    begin("y", 2)
    cross("y", 0)
    z_round(0, 2)
    z_round(1, 2)
    cross("z", 2)
    cross("z", -2)
    xy_round("x", 1)
    xy_round("y", 1)
    z_round(0, 3)
    z_round(1, 3)
    cross("z", 3)
    cross("z", -3)
    xy_round("x", 3)
    xy_round("y", 3)
    xy_round("x", 2)
    cross("x", 1)
    cross("x", -1)
    xy_round("y", 2)
    cross("y", 1)
    cross("y", -1)
    arrange("x", 0)
    arrange("y", 0)
    for piece in (0, 1):
        for axis in "xy":
            last_landed(axis, piece)
    landed("z", 0, 1, 4)
    landed("z", 1, -1, 4)
    cross("z", 4)
    for axis in "xy":
        arrange(axis, 1)
        arrange(axis, -1)
    for axis in "xy":
        last_landed(axis, 3)
    for piece in (0, 1):
        for axis in "xy":
            last_arrange(axis, piece)
    for axis in "xy":
        last_landed(axis, 2)
    arrange_z()
    for piece in (3, 2):
        for axis in "xy":
            last_arrange(axis, piece)
    second_sums()


def gather(waves, dest_of):
    count = 96
    return pl.pallas_call(
        gather_kernel,
        out_shape=[
            pltpu.VMEM((2, 4, 4, 8, 3, 16, 128), jnp.bfloat16),
            pltpu.VMEM((2, 4, 4, 8, 3, 16, 128), jnp.bfloat16),
            pltpu.VMEM((2, 8, 4, 4, 2, 16, 128), jnp.bfloat16),
            pltpu.VMEM((2, 4, 4, 8, 2, 16, 128), jnp.bfloat16),
            pltpu.VMEM((2, 4, 4, 8, 2, 16, 128), jnp.bfloat16),
            pltpu.VMEM((2, 2, 256, 128), jnp.float32),
        ],
        in_specs=[pl.BlockSpec(memory_space=pltpu.HBM)] * 2,
        out_specs=[pl.BlockSpec(memory_space=pltpu.VMEM)] * 6,
        scratch_shapes=[
            pltpu.VMEM((32, 512), jnp.bfloat16),
            pltpu.VMEM((1, 32), jnp.int32),
            pltpu.SemaphoreType.DMA((2,)),
            pltpu.SemaphoreType.DMA((count,)),
            pltpu.SemaphoreType.DMA((count,)),
        ],
        compiler_params=pltpu.CompilerParams(
            collective_id=0, has_side_effects=True, vmem_limit_bytes=24 * 2**20
        ),
    )(pltpu.with_memory_space_constraint(waves, pltpu.HBM), pltpu.with_memory_space_constraint(dest_of, pltpu.HBM))


CONTRACT = (((1,), (1,)), ((), ()))


def correlate_kernel(
    x_ref, y_ref, z_ref, sum_x, sum_y, squares, m_hbm, o_ref,
    m_ref, m_sem, even_rows, odd_rows, scale_ref, e_ref, stage, sem,
):
    blk, lag = lax.axis_index("blk"), lax.axis_index("lag")

    def shift():
        near, z, high = blk % 2, blk // 2 % 8, blk // 16

        def pick(first):
            lanes = []
            for g in range(8):
                for k in (first, first + 1):
                    x, rows = g % 4, []
                    for y in (g // 4, 2 + g // 4):
                        if k == 3:
                            rows.append(z_ref[near, z, y, x, high].astype(jnp.float32))
                        else:
                            a = x_ref[near, x, y, z, k].astype(jnp.float32)
                            b = y_ref[near, y, x, z, k].astype(jnp.float32)
                            rows.append(jnp.where(high == 0, a, b))
                    lanes.append(jnp.concatenate(rows, axis=0))
            return jnp.concatenate(lanes, axis=1)

        even, odd = pick(0), pick(2)
        mean_square = jnp.sum(even * even + odd * odd, axis=1, keepdims=True) * (1.0 / 4096)
        factor = lax.rsqrt(mean_square + EPS)
        edge = jnp.zeros((32, 256), jnp.float32)
        extend = lambda x: jnp.concatenate(
            [edge, (x * factor).astype(jnp.bfloat16).astype(jnp.float32), edge], axis=1
        )
        even, odd = extend(even), extend(odd)
        by = 2304 + 32 * lag
        before = pltpu.roll(odd, by + 1, 1)[:, :2176]
        even, odd = pltpu.roll(even, by, 1)[:, :2176], pltpu.roll(odd, by, 1)[:, :2176]
        e_ref[0] = even
        e_ref[1] = odd - even
        e_ref[2] = before - even

    def build(chunk, rows_ref):
        for q in range(8):
            for kind in (1, 2, 0):
                x = jnp.broadcast_to(e_ref[kind, 8 * chunk + q : 8 * chunk + q + 1, :], (8, 2176))
                for half in range(2):
                    y = [pltpu.roll(x, 16 * half + 8 * e, 1, stride=1, stride_axis=0)[:, 128:] for e in (0, 1)]
                    at = 32 * q + 16 * half
                    rows_ref[kind, at : at + 16, :] = jnp.concatenate(y, 0).astype(jnp.bfloat16)

    def records(q, high, g, k):
        e, near, z, y, x = q // 16, q % 2, q // 2 % 8, 2 * high + g // 4, g % 4
        if k >= 4:
            return sum_y[near, y, x, z, k - 4] if e else sum_x[near, x, y, z, k - 4]
        if k == 3:
            return z_ref[near, z, y, x, e]
        return y_ref[near, y, x, z, k] if e else x_ref[near, x, y, z, k]

    def pieces(n):
        return [(q, high) for q in range(8 * n, 8 * n + 8) for high in (0, 1)]

    def prepare(n):
        totals = []
        for q, high in pieces(n):
            at = 16 * (q % 2 * 8 + q // 2 % 8)
            totals.append(squares[q // 16, high, at : at + 16, :])
        square = lax.dot_general(
            jnp.ones((8, 128), jnp.float32), jnp.concatenate(totals, 0), CONTRACT,
            precision=lax.Precision.HIGHEST, preferred_element_type=jnp.float32,
        )
        scale_ref[:, 256 * n : 256 * n + 256] = lax.rsqrt(square * (1.0 / 4096) + EPS) * (1.0 / 64)

    def columns(n, kind, g):
        first = (4, 2, 0)[kind]
        return jnp.concatenate(
            [
                jnp.concatenate([records(q, high, g, first + k) for q, high in pieces(n)], axis=0)
                for k in (0, 1)
            ],
            axis=1,
        )

    def away(chunk, tile):
        return pltpu.make_async_copy(
            stage.at[chunk % 2, tile],
            o_ref.at[pl.ds(8 * chunk, 8), :, pl.ds(128 * tile, 128)],
            sem.at[chunk % 2, tile],
        )

    def multiply(chunk, rows_ref):
        if chunk >= 2:
            for tile in range(8):
                away(chunk - 2, tile).wait()
        for n in range(4):
            if chunk == 0:
                prepare(n)
            products = {}
            for kind in (1, 2, 0):
                right = jnp.concatenate([columns(n, kind, g) for g in range(8)], axis=1)
                products[kind] = lax.dot_general(
                    rows_ref[kind], right, CONTRACT, preferred_element_type=jnp.float32
                )
            for c in range(2):
                cols = slice(256 * n + 128 * c, 256 * n + 128 * c + 128)
                lanes = slice(128 * c, 128 * c + 128)
                for q in range(8):
                    part = slice(32 * q, 32 * q + 32)
                    a = 8 * chunk + q
                    factor = m_ref[a : a + 1, cols].astype(jnp.float32) * scale_ref[0:1, cols]
                    for p in range(2):
                        value = (products[0][part, lanes] + products[1 + p][part, lanes]) * factor
                        stage[chunk % 2, 2 * n + c, q, pl.ds(p, 32, stride=2), :] = value
                away(chunk, 2 * n + c).start()

    fetch = pltpu.make_async_copy(m_hbm, m_ref, m_sem)
    fetch.start()
    shift()
    build(0, even_rows)
    fetch.wait()
    for chunk in range(4):
        now, later = (even_rows, odd_rows) if chunk % 2 == 0 else (odd_rows, even_rows)
        if chunk < 3:
            build(chunk + 1, later)
        multiply(chunk, now)
    for chunk in (2, 3):
        for tile in range(8):
            away(chunk, tile).wait()


def correlate(gathered, pair_mask):
    return pl.pallas_call(
        correlate_kernel,
        out_shape=jax.ShapeDtypeStruct((32, 64, 1024), jnp.float32),
        in_specs=[pl.BlockSpec(memory_space=pltpu.VMEM)] * 6 + [pl.BlockSpec(memory_space=pltpu.HBM)],
        out_specs=pl.BlockSpec(memory_space=pl.ANY),
        scratch_shapes=[
            pltpu.VMEM((32, 1024), jnp.int32),
            pltpu.SemaphoreType.DMA,
            pltpu.VMEM((3, 256, 2048), jnp.bfloat16),
            pltpu.VMEM((3, 256, 2048), jnp.bfloat16),
            pltpu.VMEM((8, 1024), jnp.float32),
            pltpu.VMEM((3, 32, 2176), jnp.float32),
            pltpu.VMEM((2, 8, 8, 64, 128), jnp.float32),
            pltpu.SemaphoreType.DMA((2, 8)),
        ],
        compiler_params=pltpu.CompilerParams(vmem_limit_bytes=40 * 2**20),
    )(*gathered, pltpu.with_memory_space_constraint(pair_mask, pltpu.HBM))


def body(waves, dest_of, pair_mask):
    return correlate(gather(waves, dest_of[None, :]), pair_mask)


def solution(mesh):
    in_specs = (P("blk", "lag"), P("blk"), P("blk", None))
    out_specs = P("blk", "lag", None)
    return jax.shard_map(body, mesh=mesh, in_specs=in_specs, out_specs=out_specs, check_vma=False)
```
